32 devices in a mesh: ctx: 8 (over z, y), tp: 4 (over x, core).
Axes of the slice: x: 2, y: 2, z: 4, core: 2. Of those that a mesh axis runs over, the one named last changes fastest.
Arguments:
- query_rows: bfloat16 [2048, 64, 128], P('ctx', 'tp'), may hold values from -8 to 8
- key_rows: bfloat16 [2048, 8, 128], P('ctx', 'tp'), may hold values from -8 to 8
- value_rows: bfloat16 [2048, 8, 128], P('ctx', 'tp'), may hold values from -6 to 6
- grad_rows: bfloat16 [2048, 64, 128], P('ctx', 'tp'), may hold values from -6 to 6
- doc_ids: int32 [2048], replicated, may hold values from 0 to 8, as said below
Outputs:
- attended: bfloat16 [2048, 64, 128], P('ctx', 'tp')
- query_grad: bfloat16 [2048, 64, 128], P('ctx', 'tp')
- key_grad: bfloat16 [2048, 8, 128], P('ctx', 'tp')
- value_grad: bfloat16 [2048, 8, 128], P('ctx', 'tp')
- top_logit: float32 [], replicated
The draws below stay inside these ranges and needn't reach their ends.
Inputs may be any that keep to these rules, and one draw needn't show every extreme that they name: `doc_ids`: ids start at 0 and rise by one at each document boundary, except that the last document takes the number 4 * 2; every document holds 256 to 1024 tokens, save the last, which may be shorter; one holds exactly 1024.
All inputs are finite; a program needn't handle non-finite values.
Results may differ from the reference program's by a relative error of at most 0.018.
Values may be sent and summed in bfloat16 or wider, within the bound.
A program may use at most 128 MiB of HBM per device.

```python
import math
import jax
import jax.numpy as jnp
from jax import lax

QH = 64
KVH = 8
HD = 128
TOK_DEV = 256
DOC_MOST = 1024
TOKENS = 2048


def shared_ids(key):
    id_key = jax.random.fold_in(key, 7)
    doc_count = 4 * TOKENS // DOC_MOST + 1
    lengths = jax.random.randint(jax.random.fold_in(id_key, 1), (doc_count,), DOC_MOST // 4, DOC_MOST + 1)
    longest = jax.random.randint(jax.random.fold_in(id_key, 2), (), 0, max(doc_count // 8, 1))
    lengths = jnp.where(jnp.arange(doc_count) == longest, DOC_MOST, lengths)
    bounds = jnp.cumsum(lengths)
    raw_ids = jnp.searchsorted(bounds, jnp.arange(TOKENS), side='right').astype(jnp.int32)
    final_id = raw_ids[TOKENS - 1]
    return jnp.where(raw_ids == final_id, doc_count - 1, raw_ids).astype(jnp.int32)


def draw_doc_ids(key, part):
    return shared_ids(key)


def draw_query_rows(key, part):
    own_key = jax.random.fold_in(key, 21)
    result_rows = jnp.clip(jax.random.normal(own_key, (TOKENS, QH, HD)), -6.0, 6.0)
    return result_rows.astype(jnp.bfloat16)


def draw_key_rows(key, part):
    own_key = jax.random.fold_in(key, 31)
    result_rows = jnp.clip(jax.random.normal(own_key, (TOKENS, KVH, HD)), -6.0, 6.0)
    return result_rows.astype(jnp.bfloat16)


def block_levels(key, extent, pieces, low, top_value):
    def one(dim, blocks):
        steps = jax.random.uniform(jax.random.fold_in(jax.random.fold_in(key, 6), dim), (blocks,), jnp.float32, low / len(pieces), top_value / len(pieces))
        return jnp.repeat(jnp.exp(steps), extent[dim] // blocks).reshape((-1,) + (1,) * (len(extent) - dim - 1))

    loudness = one(*pieces[0])
    for cut in pieces[1:]:
        loudness = loudness * one(*cut)
    return loudness


def centred(key, extent, deviation, most, split=(), held_as=jnp.bfloat16):
    factor_of = block_levels(key, extent, split, -0.22, 0.18) if split else 1.0
    result = jax.random.normal(key, extent, jnp.float32) * deviation * factor_of
    return jnp.minimum(jnp.maximum(result, -most), most).astype(held_as)


def setup_inputs(seed: int = 0) -> dict:
    arg_keys = jax.random.split(jax.random.key(seed), 6)
    query_rows = draw_query_rows(jax.random.fold_in(arg_keys[5], 71), 0)
    key_rows = draw_key_rows(jax.random.fold_in(arg_keys[5], 71), 0)
    value_rows = centred(arg_keys[2], (TOKENS, KVH, HD), 1.0, 6.0, ((0, 8), (1, 4)))
    grad_rows = centred(arg_keys[3], (TOKENS, QH, HD), 1.0, 6.0, ((0, 8), (1, 4)))
    doc_ids = draw_doc_ids(jax.random.fold_in(arg_keys[5], 71), 0)
    return {"query_rows": query_rows, "key_rows": key_rows, "value_rows": value_rows, "grad_rows": grad_rows, "doc_ids": doc_ids}


def reference(query_rows, key_rows, value_rows, grad_rows, doc_ids):
    group_size = QH // KVH
    score_scale_factor = 1.0 / math.sqrt(HD)
    span_rows = DOC_MOST + TOK_DEV
    front_kv = jnp.zeros((DOC_MOST, KVH, HD), key_rows.dtype)
    key_pad = jnp.concatenate([front_kv, key_rows], 0)
    value_pad = jnp.concatenate([front_kv, value_rows], 0)
    ids_int = doc_ids.astype(jnp.int32)
    id_pad = jnp.concatenate([jnp.full((DOC_MOST,), -1, jnp.int32), ids_int], 0)
    key_place = jnp.arange(span_rows, dtype=jnp.int32)
    query_place = jnp.arange(TOK_DEV, dtype=jnp.int32) + DOC_MOST

    def one_block(state_pair, block_index):
        key_acc, value_acc = state_pair
        row_start = (block_index * TOK_DEV).astype(jnp.int32)
        query_block = lax.dynamic_slice_in_dim(query_rows, row_start, TOK_DEV, 0).astype(jnp.float32).reshape(TOK_DEV, KVH, group_size, HD)
        gradient_block = lax.dynamic_slice_in_dim(grad_rows, row_start, TOK_DEV, 0).astype(jnp.float32).reshape(TOK_DEV, KVH, group_size, HD)
        key_block = lax.dynamic_slice_in_dim(key_pad, row_start, span_rows, 0).astype(jnp.float32)
        value_block = lax.dynamic_slice_in_dim(value_pad, row_start, span_rows, 0).astype(jnp.float32)
        query_ids = lax.dynamic_slice_in_dim(ids_int, row_start, TOK_DEV, 0)
        key_ids = lax.dynamic_slice_in_dim(id_pad, row_start, span_rows, 0)
        allowed = (query_ids[:, None] == key_ids[None, :]) & (key_place[None, :] <= query_place[:, None])
        score_matrix = jnp.einsum('zeox,fex->eozf', query_block, key_block) * score_scale_factor
        masked = jnp.where(allowed[None, None], score_matrix, -jnp.inf)
        row_max = lax.optimization_barrier(jnp.max(masked, axis=-1))
        unscaled = jnp.exp(masked - row_max[..., None])
        denominator = lax.optimization_barrier(jnp.sum(unscaled, axis=-1))
        log_total = row_max + jnp.log(denominator)
        unscaled_reduced = lax.optimization_barrier(unscaled.astype(jnp.bfloat16)).astype(jnp.float32)
        attention_sum_total = jnp.einsum('ubkn,nuh->kubh', unscaled_reduced, value_block)
        norm_factor = jnp.exp(row_max - log_total)
        attended = (attention_sum_total * jnp.moveaxis(norm_factor, 2, 0)[..., None]).astype(jnp.bfloat16)
        probabilities = jnp.exp(masked - log_total[..., None])
        weights_low = probabilities.astype(jnp.bfloat16)
        weight_matrix = lax.optimization_barrier(weights_low).astype(jnp.float32)
        attended_broad_rows = attended.astype(jnp.float32)
        row_inner_product = jnp.einsum('pkvw,pkvw->kvp', gradient_block, attended_broad_rows)
        probability_gradient = jnp.einsum('zeox,fex->eozf', gradient_block, value_block)
        score_low = (probabilities * (probability_gradient - row_inner_product[..., None])).astype(jnp.bfloat16)
        score_gradient = lax.optimization_barrier(score_low).astype(jnp.float32)
        query_portion = (jnp.einsum('ubkn,nuh->kubh', score_gradient, key_block) * score_scale_factor).astype(jnp.bfloat16)
        key_portion = jnp.einsum('mjpi,pmjb->imb', score_gradient, query_block) * score_scale_factor
        value_portion = jnp.einsum('mjpi,pmjb->imb', weight_matrix, gradient_block)
        key_old = lax.dynamic_slice_in_dim(key_acc, row_start, span_rows, 0)
        value_old = lax.dynamic_slice_in_dim(value_acc, row_start, span_rows, 0)
        key_acc = lax.dynamic_update_slice_in_dim(key_acc, key_old + key_portion, row_start, 0)
        value_acc = lax.dynamic_update_slice_in_dim(value_acc, value_old + value_portion, row_start, 0)
        outputs = (attended.reshape(TOK_DEV, QH, HD), query_portion.reshape(TOK_DEV, QH, HD), jnp.max(row_max))
        return ((key_acc, value_acc), outputs)
    zero_acc = jnp.zeros((DOC_MOST + TOKENS, KVH, HD), jnp.float32)
    block_list = jnp.arange(TOKENS // TOK_DEV, dtype=jnp.int32)
    final_pair, stacked = lax.scan(one_block, (zero_acc, zero_acc), block_list)
    key_acc, value_acc = final_pair
    attended = stacked[0].reshape(TOKENS, QH, HD)
    query_grad = stacked[1].reshape(TOKENS, QH, HD)
    top_logit = jnp.max(stacked[2])
    key_grad = key_acc[DOC_MOST:].astype(jnp.bfloat16)
    value_grad = value_acc[DOC_MOST:].astype(jnp.bfloat16)
    return (attended, query_grad, key_grad, value_grad, top_logit)
```

```python
import functools
import math

import jax
import jax.numpy as jnp
from jax import lax
from jax.experimental import pallas as pl
from jax.experimental.pallas import tpu as pltpu
from jax.sharding import PartitionSpec as P

REACH = 4
ROWS = 256
NEGATIVE = -1e30
F32 = jnp.float32
BF16 = jnp.bfloat16
NT = (((1,), (1,)), ((), ()))


def shift(block, distance):
    devices = range(lax.axis_size("ctx"))
    route = [(i, i + distance) for i in devices if i + distance in devices]
    return lax.ppermute(block, "ctx", route)


def chunk_step(
    c, peak, g, heads, tokens, q_ref, do_ref, lo_ref, k_ref, v_ref, kt_ref, vt_ref,
    o_ref, dq_ref, dk_ref, dv_ref, s_ref, dp_ref, w_ref, ds_ref,
):
    tiles = k_ref.shape[1] // tokens
    width = k_ref.shape[2]
    scale = 1.0 / math.sqrt(width)
    base2 = scale * math.log2(math.e)
    rows = pl.ds(pl.multiple_of(c * ROWS, ROWS), ROWS)
    q = q_ref[g, rows, :]
    do = do_ref[g, rows, :]
    low = lo_ref[:, rows]
    key_place = lax.broadcasted_iota(jnp.int32, (tokens, ROWS), 0)
    query_place = (lax.broadcasted_iota(jnp.int32, (1, ROWS), 1) + c * ROWS) // heads
    top = jnp.full((1, ROWS), NEGATIVE, F32)
    for j in range(tiles):
        keys = pl.ds(j * tokens, tokens)
        s = lax.dot_general(k_ref[g, keys, :], q, NT, preferred_element_type=F32)
        allowed = key_place >= low + j * tokens
        if j == 0:
            allowed = allowed & (key_place <= query_place)
        s = jnp.where(allowed, s, NEGATIVE)
        s_ref[keys, :] = s
        top = jnp.maximum(top, jnp.max(s, axis=0, keepdims=True))
    total = jnp.zeros((1, ROWS), F32)
    dot = jnp.zeros((1, ROWS), F32)
    for j in range(tiles):
        keys = pl.ds(j * tokens, tokens)
        p = jnp.exp2((s_ref[keys, :] - top) * base2)
        dp = lax.dot_general(v_ref[g, keys, :], do, NT, preferred_element_type=F32)
        s_ref[keys, :] = p
        dp_ref[keys, :] = dp
        total = total + jnp.sum(p, axis=0, keepdims=True)
        dot = dot + jnp.sum(p * dp, axis=0, keepdims=True)
    inverse = 1.0 / total
    dot = dot * inverse
    for j in range(tiles):
        keys = pl.ds(j * tokens, tokens)
        p = s_ref[keys, :] * inverse
        w_ref[keys, :] = p.astype(BF16)
        ds_ref[keys, :] = (p * (dp_ref[keys, :] - dot)).astype(BF16)
    w = w_ref[...]
    ds = ds_ref[...]
    o = jnp.dot(vt_ref[...], w, preferred_element_type=F32)
    dq = jnp.dot(kt_ref[...], ds, preferred_element_type=F32) * scale
    o_ref[g, rows, :] = o.T.astype(BF16)
    dq_ref[g, rows, :] = dq.T.astype(BF16)
    dv_ref[...] += jnp.dot(w, do, preferred_element_type=F32)
    dk_ref[...] += jnp.dot(ds, q, preferred_element_type=F32)
    return jnp.maximum(peak, top)


def kernel(
    heads, tokens, q_ref, do_ref, lo_ref, k_ref, v_ref,
    o_ref, dq_ref, dk_out, dv_out, top_ref,
    kt_ref, vt_ref, dk_ref, dv_ref, s_ref, dp_ref, w_ref, ds_ref,
):
    groups, rows, width = q_ref.shape
    scale = 1.0 / math.sqrt(width)
    peak = jnp.full((1, ROWS), NEGATIVE, F32)
    for g in range(groups):
        kt_ref[...] = k_ref[g].T
        vt_ref[...] = v_ref[g].T
        dk_ref[...] = jnp.zeros_like(dk_ref)
        dv_ref[...] = jnp.zeros_like(dv_ref)
        step = functools.partial(
            chunk_step, g=g, heads=heads, tokens=tokens, q_ref=q_ref, do_ref=do_ref,
            lo_ref=lo_ref, k_ref=k_ref, v_ref=v_ref, kt_ref=kt_ref, vt_ref=vt_ref,
            o_ref=o_ref, dq_ref=dq_ref, dk_ref=dk_ref, dv_ref=dv_ref, s_ref=s_ref,
            dp_ref=dp_ref, w_ref=w_ref, ds_ref=ds_ref,
        )
        peak = lax.fori_loop(0, rows // ROWS, step, peak)
        dk_out[g] = (dk_ref[...] * scale).astype(BF16)
        dv_out[g] = dv_ref[...].astype(BF16)
    top_ref[...] = jnp.broadcast_to(jnp.max(peak, axis=1, keepdims=True) * scale, top_ref.shape)


def shards(query_rows, key_rows, value_rows, grad_rows, doc_ids):
    tokens, head_count, width = query_rows.shape
    groups = key_rows.shape[1]
    heads = head_count // groups
    me = lax.axis_index("ctx")
    own_ids = lax.dynamic_slice_in_dim(doc_ids, me * tokens, tokens, 0)
    first = jnp.sum((doc_ids[None, :] < own_ids[:, None]).astype(jnp.int32), axis=1)
    low = jnp.repeat(first - me * tokens, heads)[None, :]

    def by_group(x):
        return x.reshape(tokens, groups, heads, width).transpose(1, 0, 2, 3).reshape(groups, tokens * heads, width)

    def by_token(x):
        return x.reshape(groups, tokens, heads, width).transpose(1, 0, 2, 3).reshape(tokens, head_count, width)

    own = jnp.stack([key_rows, value_rows]).transpose(0, 2, 1, 3)
    blocks = [own] + [shift(own, d) for d in range(1, REACH + 1)]
    both = jnp.concatenate(blocks, axis=2)
    keys = both.shape[2]
    vmem = pl.BlockSpec(memory_space=pltpu.VMEM)
    attended, query_grad, dk, dv, top = pl.pallas_call(
        functools.partial(kernel, heads, tokens),
        out_shape=(
            jax.ShapeDtypeStruct((groups, tokens * heads, width), BF16),
            jax.ShapeDtypeStruct((groups, tokens * heads, width), BF16),
            jax.ShapeDtypeStruct((groups, keys, width), BF16),
            jax.ShapeDtypeStruct((groups, keys, width), BF16),
            jax.ShapeDtypeStruct((8, 128), F32),
        ),
        in_specs=[vmem] * 5,
        out_specs=(vmem,) * 5,
        scratch_shapes=[
            pltpu.VMEM((width, keys), BF16),
            pltpu.VMEM((width, keys), BF16),
            pltpu.VMEM((keys, width), F32),
            pltpu.VMEM((keys, width), F32),
            pltpu.VMEM((keys, ROWS), F32),
            pltpu.VMEM((keys, ROWS), F32),
            pltpu.VMEM((keys, ROWS), BF16),
            pltpu.VMEM((keys, ROWS), BF16),
        ],
        compiler_params=pltpu.CompilerParams(vmem_limit_bytes=50 << 20),
    )(by_group(query_rows), by_group(grad_rows), low, both[0], both[1])
    parts = jnp.stack([dk, dv]).reshape(2, groups, REACH + 1, tokens, width)
    result = parts[:, :, 0].astype(F32)
    for d in range(1, REACH + 1):
        result = result + shift(parts[:, :, d], -d).astype(F32)
    result = result.transpose(0, 2, 1, 3).astype(BF16)
    top_logit = lax.pmax(top[0, 0], ("ctx", "tp"))
    return by_token(attended), by_token(query_grad), result[0], result[1], top_logit


def solution(mesh):
    part = P("ctx", "tp", None)
    return jax.shard_map(
        shards,
        mesh=mesh,
        in_specs=(part, part, part, part, P()),
        out_specs=(part, part, part, part, P()),
        check_vma=False,
    )
```

```python
import functools
import math

import jax
import jax.numpy as jnp
from jax import lax
from jax.experimental import pallas as pl
from jax.experimental.pallas import tpu as pltpu
from jax.sharding import PartitionSpec as P

REACH = 4
ROWS = 256
NEGATIVE = -1e30
F32 = jnp.float32
BF16 = jnp.bfloat16
NT = (((1,), (1,)), ((), ()))


def chunk_step(
    c, peak, g, heads, tokens, q_ref, do_ref, lo_ref, kv_ref, kt_ref, vt_ref,
    o_ref, dq_ref, dk_ref, dv_ref, s_ref, dp_ref, w_ref, ds_ref,
):
    tiles, width = kv_ref.shape[1], kv_ref.shape[4]
    scale = 1.0 / math.sqrt(width)
    base2 = scale * math.log2(math.e)
    rows = pl.ds(pl.multiple_of(c * ROWS, ROWS), ROWS)
    q = q_ref[g, rows, :]
    do = do_ref[g, rows, :]
    low = lo_ref[:, rows]
    key_place = lax.broadcasted_iota(jnp.int32, (tokens, ROWS), 0)
    query_place = (lax.broadcasted_iota(jnp.int32, (1, ROWS), 1) + c * ROWS) // heads
    top = jnp.full((1, ROWS), NEGATIVE, F32)
    for j in range(tiles):
        keys = pl.ds(j * tokens, tokens)
        s = lax.dot_general(kv_ref[g, j, 0], q, NT, preferred_element_type=F32)
        allowed = key_place >= low + j * tokens
        if j == 0:
            allowed = allowed & (key_place <= query_place)
        s = jnp.where(allowed, s, NEGATIVE)
        s_ref[keys, :] = s
        top = jnp.maximum(top, jnp.max(s, axis=0, keepdims=True))
    total = jnp.zeros((1, ROWS), F32)
    dot = jnp.zeros((1, ROWS), F32)
    for j in range(tiles):
        keys = pl.ds(j * tokens, tokens)
        p = jnp.exp2((s_ref[keys, :] - top) * base2)
        dp = lax.dot_general(kv_ref[g, j, 1], do, NT, preferred_element_type=F32)
        s_ref[keys, :] = p
        dp_ref[keys, :] = dp
        total = total + jnp.sum(p, axis=0, keepdims=True)
        dot = dot + jnp.sum(p * dp, axis=0, keepdims=True)
    inverse = 1.0 / total
    dot = dot * inverse
    for j in range(tiles):
        keys = pl.ds(j * tokens, tokens)
        p = s_ref[keys, :] * inverse
        w_ref[keys, :] = p.astype(BF16)
        ds_ref[keys, :] = (p * (dp_ref[keys, :] - dot)).astype(BF16)
    w = w_ref[...]
    ds = ds_ref[...]
    o = jnp.dot(vt_ref[...], w, preferred_element_type=F32)
    dq = jnp.dot(kt_ref[...], ds, preferred_element_type=F32) * scale
    o_ref[g, rows, :] = o.T.astype(BF16)
    dq_ref[g, rows, :] = dq.T.astype(BF16)
    dv_ref[...] += jnp.dot(w, do, preferred_element_type=F32)
    dk_ref[...] += jnp.dot(ds, q, preferred_element_type=F32)
    return jnp.maximum(peak, top)


def kernel(
    heads, tokens, sizes, q_ref, do_ref, lo_ref, own_ref,
    o_ref, dq_ref, dkv_ref, top_ref,
    kv_ref, out_ref, back_ref, peak_ref, peer_ref, kt_ref, vt_ref, dk_ref, dv_ref,
    s_ref, dp_ref, w_ref, ds_ref, send_sem, recv_sem, peak_send, peak_recv,
):
    groups, rows, width = q_ref.shape
    ranks, lanes = sizes
    chunks = rows // ROWS
    scale = 1.0 / math.sqrt(width)
    me = lax.axis_index("ctx")
    lane = lax.axis_index("tp")
    odd = lax.rem(me, 2) == 1
    even = lax.rem(me, 2) == 0
    mate = me + 1 - 2 * lax.rem(me, 2)
    has_ahead = me + 2 < ranks

    def flip(index, bit):
        return index + bit - 2 * bit * lax.rem(index // bit, 2)

    peers = [("ctx", flip(me, 1 << b)) for b in range((ranks - 1).bit_length())]
    peers += [("tp", flip(lane, 1 << b)) for b in range((lanes - 1).bit_length())]
    barrier = pltpu.get_barrier_semaphore()

    def greet(axis, index):
        pl.semaphore_signal(barrier, inc=1, device_id={axis: index}, device_id_type=pl.DeviceIdType.MESH)

    for axis, index in peers:
        greet(axis, index)
    pl.when(has_ahead)(lambda: greet("ctx", me + 2))
    pl.when(me >= 2)(lambda: greet("ctx", me - 2))
    pl.semaphore_wait(barrier, len(peers) + has_ahead.astype(jnp.int32) + (me >= 2).astype(jnp.int32))

    def move(g, k, src, dst, target):
        return pltpu.make_async_remote_copy(
            src_ref=src, dst_ref=dst, send_sem=send_sem.at[g, k], recv_sem=recv_sem.at[g, k],
            device_id={"ctx": target}, device_id_type=pl.DeviceIdType.MESH,
        )

    def hops(g):
        kv = lambda j: kv_ref.at[g, j]
        out = lambda k: out_ref.at[g, k]
        back = lambda k: back_ref.at[g, k]
        return {
            "a": (0, [(has_ahead, own_ref.at[g])], kv(2), me + 2, me >= 2),
            "b": (1, [(has_ahead & (me >= 2), kv(2))], kv(4), me + 2, me >= 4),
            "y1": (2, [(even, own_ref.at[g]), (odd & (me >= 3), kv(2))], kv(1), mate, me >= 1),
            "y3e": (3, [(even & (me >= 2), kv(2))], kv(3), mate, odd & (me >= 3)),
            "y3o": (4, [(odd & (me >= 5), kv(4))], kv(3), mate, even & (me >= 4)),
            "d1": (5, [(me >= 1, out(0))], back(0), mate, even | (me >= 3)),
            "d3": (6, [(me >= 3, out(2))], back(2), mate, (even & (me >= 2)) | (me >= 5)),
            "d4": (7, [(me >= 4, out(3))], back(3), me - 2, has_ahead & (me >= 2)),
            "d2": (8, [(me >= 2, out(1))], back(1), me - 2, has_ahead),
        }

    def start(g, name):
        slot, sources, dst, target, _ = hops(g)[name]
        for cond, src in sources:
            pl.when(cond)(lambda src=src: move(g, slot, src, dst, target).start())

    def arrive(g, name):
        slot, sources, dst, target, cond = hops(g)[name]
        pl.when(cond)(lambda: move(g, slot, sources[0][1], dst, target).wait_recv())

    def sent(g, name):
        slot, sources, dst, target, _ = hops(g)[name]
        for cond, src in sources:
            pl.when(cond)(lambda src=src: move(g, slot, src, dst, target).wait_send())

    def add(k, cond, g, slot):
        keys = pl.ds(k * tokens, tokens)

        @pl.when(cond)
        def _():
            dk_ref[g, keys, :] += back_ref[g, slot, 0].astype(F32)
            dv_ref[g, keys, :] += back_ref[g, slot, 1].astype(F32)

    def pack(g, k):
        keys = pl.ds(k * tokens, tokens)
        out_ref[g, k - 1, 0] = dk_ref[g, keys, :].astype(BF16)
        out_ref[g, k - 1, 1] = dv_ref[g, keys, :].astype(BF16)

    def back_one(g):
        pack(g, 1)
        pack(g, 3)
        start(g, "d3")
        start(g, "d1")

    def back_two(g):
        arrive(g, "d3")
        add(4, odd & (me >= 5), g, 2)
        add(2, even & (me >= 2), g, 2)
        pack(g, 4)
        start(g, "d4")

    def back_three(g):
        arrive(g, "d1")
        add(2, odd & (me >= 3), g, 0)
        add(0, even, g, 0)
        arrive(g, "d4")
        add(2, has_ahead & (me >= 2), g, 3)
        pack(g, 2)
        start(g, "d2")

    def back_last(g):
        arrive(g, "d2")
        add(0, has_ahead, g, 1)
        keys = pl.ds(0, tokens)
        dkv_ref[g, 0] = (dk_ref[g, keys, :] * scale).astype(BF16)
        dkv_ref[g, 1] = dv_ref[g, keys, :].astype(BF16)

    for g in range(groups):
        start(g, "a")
    for g in range(groups):
        pl.when(even)(lambda g=g: move(g, 2, own_ref.at[g], kv_ref.at[g, 1], mate).start())
    for g in range(groups):
        kv_ref[g, 0] = own_ref[g]
        for j in range(1, REACH + 1):
            @pl.when(me < j)
            def _(g=g, j=j):
                kv_ref[g, j] = jnp.zeros_like(kv_ref[g, j])
    dk_ref[...] = jnp.zeros_like(dk_ref)
    dv_ref[...] = jnp.zeros_like(dv_ref)
    for g in range(groups):
        arrive(g, "a")
        start(g, "b")
        pl.when(odd & (me >= 3))(lambda g=g: move(g, 2, kv_ref.at[g, 2], kv_ref.at[g, 1], mate).start())
        start(g, "y3e")
    def ready(g):
        arrive(g, "b")
        start(g, "y3o")
    def begin(g):
        for name in ("y1", "y3e", "y3o"):
            arrive(g, name)
        for j in range(REACH + 1):
            keys = pl.ds(j * tokens, tokens)
            kt_ref[:, keys] = kv_ref[g, j, 0].T
            vt_ref[:, keys] = kv_ref[g, j, 1].T
    ready(0)
    peak = jnp.full((1, ROWS), NEGATIVE, F32)
    plan = {(0, 0): [lambda: begin(0)]}
    for g in range(1, groups):
        plan.setdefault((g - 1, 3), []).append(lambda g=g: ready(g))
        plan.setdefault((g, 0), []).append(lambda g=g: (back_one(g - 1), begin(g)))
        plan.setdefault((g, 2), []).append(lambda g=g: back_two(g - 1))
        plan.setdefault((g, 4), []).append(lambda g=g: back_three(g - 1))
        plan.setdefault((g, 6), []).append(lambda g=g: back_last(g - 1))

    def step(t, peak):
        for (g, c), works in plan.items():
            @pl.when(t == g * chunks + c)
            def _(works=works):
                for work in works:
                    work()
        g = t // chunks
        return chunk_step(
            t - g * chunks, peak, g=g, heads=heads, tokens=tokens, q_ref=q_ref, do_ref=do_ref,
            lo_ref=lo_ref, kv_ref=kv_ref, kt_ref=kt_ref, vt_ref=vt_ref,
            o_ref=o_ref, dq_ref=dq_ref, dk_ref=dk_ref.at[g], dv_ref=dv_ref.at[g], s_ref=s_ref,
            dp_ref=dp_ref, w_ref=w_ref, ds_ref=ds_ref,
        )

    peak = lax.fori_loop(0, groups * chunks, step, peak)
    last = groups - 1
    back_one(last)
    best = jnp.broadcast_to(jnp.max(peak, axis=1, keepdims=True) * scale, top_ref.shape)

    def swap(r):
        axis, index = peers[r]
        return pltpu.make_async_remote_copy(
            src_ref=peak_ref.at[r], dst_ref=peer_ref.at[r], send_sem=peak_send.at[r],
            recv_sem=peak_recv.at[r], device_id={axis: index}, device_id_type=pl.DeviceIdType.MESH,
        )

    after = {1: back_two, 3: back_three}
    for r in range(len(peers)):
        peak_ref[r] = best
        swap(r).start()
        if r in after:
            after[r](last)
        swap(r).wait_recv()
        best = jnp.maximum(best, peer_ref[r])
    top_ref[...] = best
    back_last(last)
    for r in range(len(peers)):
        swap(r).wait_send()
    for g in range(groups):
        for name in ("a", "b", "y1", "y3e", "y3o", "d1", "d3", "d4", "d2"):
            sent(g, name)


def shards(sizes, query_rows, key_rows, value_rows, grad_rows, doc_ids):
    tokens, head_count, width = query_rows.shape
    groups = key_rows.shape[1]
    heads = head_count // groups
    me = lax.axis_index("ctx")
    own_ids = lax.dynamic_slice_in_dim(doc_ids, me * tokens, tokens, 0)
    first = jnp.sum((doc_ids[None, :] < own_ids[:, None]).astype(jnp.int32), axis=1)
    low = jnp.repeat(first - me * tokens, heads)[None, :]

    def by_group(x):
        return x.reshape(tokens, groups, heads, width).transpose(1, 0, 2, 3).reshape(groups, tokens * heads, width)

    def by_token(x):
        return x.reshape(groups, tokens, heads, width).transpose(1, 0, 2, 3).reshape(tokens, head_count, width)

    own = jnp.stack([key_rows, value_rows]).transpose(2, 0, 1, 3)
    tiles = REACH + 1
    keys = tiles * tokens
    rounds = sum((size - 1).bit_length() for size in sizes)
    vmem = pl.BlockSpec(memory_space=pltpu.VMEM)
    attended, query_grad, dkv, top = pl.pallas_call(
        functools.partial(kernel, heads, tokens, sizes),
        out_shape=(
            jax.ShapeDtypeStruct((groups, tokens * heads, width), BF16),
            jax.ShapeDtypeStruct((groups, tokens * heads, width), BF16),
            jax.ShapeDtypeStruct((groups, 2, tokens, width), BF16),
            jax.ShapeDtypeStruct((8, 128), F32),
        ),
        in_specs=[vmem] * 4,
        out_specs=(vmem,) * 4,
        scratch_shapes=[
            pltpu.VMEM((groups, tiles, 2, tokens, width), BF16),
            pltpu.VMEM((groups, REACH, 2, tokens, width), BF16),
            pltpu.VMEM((groups, REACH, 2, tokens, width), BF16),
            pltpu.VMEM((rounds, 8, 128), F32),
            pltpu.VMEM((rounds, 8, 128), F32),
            pltpu.VMEM((width, keys), BF16),
            pltpu.VMEM((width, keys), BF16),
            pltpu.VMEM((groups, keys, width), F32),
            pltpu.VMEM((groups, keys, width), F32),
            pltpu.VMEM((keys, ROWS), F32),
            pltpu.VMEM((keys, ROWS), F32),
            pltpu.VMEM((keys, ROWS), BF16),
            pltpu.VMEM((keys, ROWS), BF16),
            pltpu.SemaphoreType.DMA((groups, 9)),
            pltpu.SemaphoreType.DMA((groups, 9)),
            pltpu.SemaphoreType.DMA((rounds,)),
            pltpu.SemaphoreType.DMA((rounds,)),
        ],
        compiler_params=pltpu.CompilerParams(
            vmem_limit_bytes=50 << 20, collective_id=0, has_side_effects=True
        ),
    )(by_group(query_rows), by_group(grad_rows), low, own)
    result = dkv.transpose(1, 2, 0, 3)
    return by_token(attended), by_token(query_grad), result[0], result[1], top[0, 0]


def solution(mesh):
    part = P("ctx", "tp", None)
    return jax.shard_map(
        functools.partial(shards, (mesh.shape["ctx"], mesh.shape["tp"])),
        mesh=mesh,
        in_specs=(part, part, part, part, P()),
        out_specs=(part, part, part, part, P()),
        check_vma=False,
    )
```

```python
import functools
import math

import jax
import jax.numpy as jnp
from jax import lax
from jax.experimental import pallas as pl
from jax.experimental.pallas import tpu as pltpu
from jax.sharding import PartitionSpec as P

REACH = 4
ROWS = 256
FILL = 512
NEGATIVE = -1e30
F32 = jnp.float32
BF16 = jnp.bfloat16
NT = (((1,), (1,)), ((), ()))


def fill(g, j, heads, tokens, q_ref, do_ref, lo_ref, kv_ref, kt_ref, vt_ref, s_ref, dp_ref, max_ref):
    keys = pl.ds(j * tokens, tokens)
    kt_ref[:, keys] = kv_ref[g, j, 0].T
    vt_ref[:, keys] = kv_ref[g, j, 1].T
    key_place = lax.broadcasted_iota(jnp.int32, (tokens, FILL), 0)

    def body(c, carry):
        rows = pl.ds(pl.multiple_of(c * FILL, FILL), FILL)
        s = lax.dot_general(kv_ref[g, j, 0], q_ref[g, rows, :], NT, preferred_element_type=F32)
        allowed = key_place >= lo_ref[:, rows] + j * tokens
        if j == 0:
            query_place = (lax.broadcasted_iota(jnp.int32, (1, FILL), 1) + c * FILL) // heads
            allowed = allowed & (key_place <= query_place)
        s = jnp.where(allowed, s, NEGATIVE)
        s_ref[keys, rows] = s
        top = jnp.max(s, axis=0, keepdims=True)
        max_ref[:, rows] = top if j == 0 else jnp.maximum(max_ref[:, rows], top)
        dp_ref[keys, rows] = lax.dot_general(
            kv_ref[g, j, 1], do_ref[g, rows, :], NT, preferred_element_type=F32
        )
        return carry

    lax.fori_loop(0, q_ref.shape[1] // FILL, body, 0)


def chunk_step(
    c, g, tokens, o_ref, dq_ref, kt_ref, vt_ref, s_ref, dp_ref, w_ref, ds_ref, max_ref
):
    width = kt_ref.shape[0]
    tiles = kt_ref.shape[1] // tokens
    scale = 1.0 / math.sqrt(width)
    base2 = scale * math.log2(math.e)
    rows = pl.ds(pl.multiple_of(c * ROWS, ROWS), ROWS)
    top = max_ref[:, rows]
    total = jnp.zeros((1, ROWS), F32)
    dot = jnp.zeros((1, ROWS), F32)
    for j in range(tiles):
        keys = pl.ds(j * tokens, tokens)
        p = jnp.exp2((s_ref[keys, rows] - top) * base2)
        s_ref[keys, rows] = p
        total = total + jnp.sum(p, axis=0, keepdims=True)
        dot = dot + jnp.sum(p * dp_ref[keys, rows], axis=0, keepdims=True)
    inverse = 1.0 / total
    dot = dot * inverse
    for j in range(tiles):
        keys = pl.ds(j * tokens, tokens)
        p = s_ref[keys, rows] * inverse
        w_ref[keys, rows] = p.astype(BF16)
        ds_ref[keys, rows] = (p * (dp_ref[keys, rows] - dot)).astype(BF16)
    o = jnp.dot(vt_ref[...], w_ref[:, rows], preferred_element_type=F32)
    dq = jnp.dot(kt_ref[...], ds_ref[:, rows], preferred_element_type=F32) * scale
    o_ref[g, rows, :] = o.T.astype(BF16)
    dq_ref[g, rows, :] = dq.T.astype(BF16)


def kernel(
    heads, tokens, sizes, q_ref, do_ref, lo_ref, own_ref,
    o_ref, dq_ref, dkv_ref, top_ref,
    kv_ref, out_ref, back_ref, peak_ref, peer_ref, kt_ref, vt_ref, dk_ref, dv_ref,
    s_ref, dp_ref, w_ref, ds_ref, max_ref, best_ref, send_sem, recv_sem, peak_send, peak_recv,
):
    groups, rows, width = q_ref.shape
    ranks, lanes = sizes
    chunks = rows // ROWS
    scale = 1.0 / math.sqrt(width)
    me = lax.axis_index("ctx")
    lane = lax.axis_index("tp")
    odd = lax.rem(me, 2) == 1
    even = lax.rem(me, 2) == 0
    mate = me + 1 - 2 * lax.rem(me, 2)
    has_ahead = me + 2 < ranks

    def flip(index, bit):
        return index + bit - 2 * bit * lax.rem(index // bit, 2)

    peers = [("ctx", flip(me, 1 << b)) for b in range((ranks - 1).bit_length())]
    peers += [("tp", flip(lane, 1 << b)) for b in range((lanes - 1).bit_length())]
    barrier = pltpu.get_barrier_semaphore()

    def greet(axis, index):
        pl.semaphore_signal(barrier, inc=1, device_id={axis: index}, device_id_type=pl.DeviceIdType.MESH)

    for axis, index in peers:
        greet(axis, index)
    pl.when(has_ahead)(lambda: greet("ctx", me + 2))
    pl.when(me >= 2)(lambda: greet("ctx", me - 2))
    pl.semaphore_wait(barrier, len(peers) + has_ahead.astype(jnp.int32) + (me >= 2).astype(jnp.int32))

    def move(g, k, src, dst, target):
        return pltpu.make_async_remote_copy(
            src_ref=src, dst_ref=dst, send_sem=send_sem.at[g, k], recv_sem=recv_sem.at[g, k],
            device_id={"ctx": target}, device_id_type=pl.DeviceIdType.MESH,
        )

    def hops(g):
        kv = lambda j: kv_ref.at[g, j]
        out = lambda k: out_ref.at[g, k]
        back = lambda k: back_ref.at[g, k]
        return {
            "a": (0, [(has_ahead, own_ref.at[g])], kv(2), me + 2, me >= 2),
            "b": (1, [(has_ahead & (me >= 2), kv(2))], kv(4), me + 2, me >= 4),
            "y1": (2, [(even, own_ref.at[g]), (odd & (me >= 3), kv(2))], kv(1), mate, me >= 1),
            "y3e": (3, [(even & (me >= 2), kv(2))], kv(3), mate, odd & (me >= 3)),
            "y3o": (4, [(odd & (me >= 5), kv(4))], kv(3), mate, even & (me >= 4)),
            "d1": (5, [(me >= 1, out(0))], back(0), mate, even | (me >= 3)),
            "d3": (6, [(me >= 3, out(2))], back(2), mate, (even & (me >= 2)) | (me >= 5)),
            "d4": (7, [(me >= 4, out(3))], back(3), me - 2, has_ahead & (me >= 2)),
            "d2": (8, [(me >= 2, out(1))], back(1), me - 2, has_ahead),
        }

    def start(g, name):
        slot, sources, dst, target, _ = hops(g)[name]
        for cond, src in sources:
            pl.when(cond)(lambda src=src: move(g, slot, src, dst, target).start())

    def arrive(g, name):
        slot, sources, dst, target, cond = hops(g)[name]
        pl.when(cond)(lambda: move(g, slot, sources[0][1], dst, target).wait_recv())

    def sent(g, name):
        slot, sources, dst, target, _ = hops(g)[name]
        for cond, src in sources:
            pl.when(cond)(lambda src=src: move(g, slot, src, dst, target).wait_send())

    def add(k, cond, g, slot):
        keys = pl.ds(k * tokens, tokens)

        @pl.when(cond)
        def _():
            dk_ref[g, keys, :] += back_ref[g, slot, 0].astype(F32)
            dv_ref[g, keys, :] += back_ref[g, slot, 1].astype(F32)

    def pack(g, k):
        keys = pl.ds(k * tokens, tokens)
        out_ref[g, k - 1, 0] = dk_ref[g, keys, :].astype(BF16)
        out_ref[g, k - 1, 1] = dv_ref[g, keys, :].astype(BF16)

    def finish(g, j):
        keys = pl.ds(j * tokens, tokens)
        dv_ref[g, keys, :] = jnp.dot(w_ref[keys, :], do_ref[g], preferred_element_type=F32)
        dk_ref[g, keys, :] = jnp.dot(ds_ref[keys, :], q_ref[g], preferred_element_type=F32)

    def back_two(g):
        arrive(g, "d3")
        add(4, odd & (me >= 5), g, 2)
        pack(g, 4)
        start(g, "d4")

    def back_three(g):
        arrive(g, "d1")
        add(2, even & (me >= 2), g, 2)
        add(2, odd & (me >= 3), g, 0)
        arrive(g, "d4")
        add(2, has_ahead & (me >= 2), g, 3)
        pack(g, 2)
        start(g, "d2")

    def back_last(g):
        add(0, even, g, 0)
        arrive(g, "d2")
        add(0, has_ahead, g, 1)
        keys = pl.ds(0, tokens)
        dkv_ref[g, 0] = (dk_ref[g, keys, :] * scale).astype(BF16)
        dkv_ref[g, 1] = dv_ref[g, keys, :].astype(BF16)

    def begin(g):
        start(g, "a")
        pl.when(even)(lambda: move(g, 2, own_ref.at[g], kv_ref.at[g, 1], mate).start())

    def relay(g):
        arrive(g, "a")
        start(g, "b")
        pl.when(odd & (me >= 3))(lambda: move(g, 2, kv_ref.at[g, 2], kv_ref.at[g, 1], mate).start())
        start(g, "y3e")

    def relay_last(g):
        arrive(g, "b")
        start(g, "y3o")

    def swap(r):
        axis, index = peers[r]
        return pltpu.make_async_remote_copy(
            src_ref=peak_ref.at[r], dst_ref=peer_ref.at[r], send_sem=peak_send.at[r],
            recv_sem=peak_recv.at[r], device_id={axis: index}, device_id_type=pl.DeviceIdType.MESH,
        )

    def collect(r):
        if r > 0:
            swap(r - 1).wait_recv()
            best_ref[...] = jnp.maximum(best_ref[...], peer_ref[r - 1])
        if r < len(peers):
            peak_ref[r] = best_ref[...]
            swap(r).start()

    def fill_tile(g, j):
        fill(g, j, heads, tokens, q_ref, do_ref, lo_ref, kv_ref, kt_ref, vt_ref, s_ref, dp_ref, max_ref)

    def note_peak():
        best = jnp.max(max_ref[...], axis=1, keepdims=True) * scale
        best_ref[...] = jnp.maximum(best_ref[...], jnp.broadcast_to(best, best_ref.shape))

    def main(g, plan):
        def step(c, carry):
            for at, works in plan.items():
                @pl.when(c == at)
                def _(works=works):
                    for work in works:
                        work()
            chunk_step(c, g, tokens, o_ref, dq_ref, kt_ref, vt_ref, s_ref, dp_ref, w_ref, ds_ref, max_ref)
            return carry

        lax.fori_loop(0, chunks, step, 0)

    begin(0)
    best_ref[...] = jnp.full_like(best_ref, NEGATIVE)
    for g in range(groups):
        kv_ref[g, 0] = own_ref[g]
        for j in range(1, REACH + 1):
            @pl.when(me < j)
            def _(g=g, j=j):
                kv_ref[g, j] = jnp.zeros_like(kv_ref[g, j])
    last = groups - 1
    for g in range(groups):
        fill_tile(g, 0)
        if g == 0:
            relay(0)
            fill_tile(0, 2)
            arrive(0, "y1")
            fill_tile(0, 1)
            relay_last(0)
            if last > 0:
                begin(1)
            fill_tile(0, 4)
            arrive(0, "y3e")
            arrive(0, "y3o")
            fill_tile(0, 3)
        else:
            fill_tile(g, 2)
            arrive(g, "y1")
            fill_tile(g, 1)
            back_two(g - 1)
            fill_tile(g, 4)
            arrive(g, "y3e")
            arrive(g, "y3o")
            fill_tile(g, 3)
        note_peak()
        plan = {}
        if g > 0:
            plan.setdefault(1, []).append(lambda g=g: back_three(g - 1))
            plan.setdefault(4, []).append(lambda g=g: back_last(g - 1))
        if g < last:
            plan.setdefault(2, []).append(lambda g=g: relay(g + 1))
            plan.setdefault(5, []).append(lambda g=g: relay_last(g + 1))
            if g + 1 < last:
                plan.setdefault(6, []).append(lambda g=g: begin(g + 2))
        else:
            for r in range(min(len(peers) + 1, chunks)):
                plan.setdefault(r, []).append(lambda r=r: collect(r))
        main(g, plan)
        finish(g, 3)
        pack(g, 3)
        start(g, "d3")
        finish(g, 1)
        pack(g, 1)
        start(g, "d1")
        finish(g, 4)
        if g == last:
            back_two(g)
        finish(g, 2)
        if g == last:
            back_three(g)
        finish(g, 0)
    for r in range(chunks, len(peers) + 1):
        collect(r)
    top_ref[...] = best_ref[...]
    back_last(last)
    for r in range(len(peers)):
        swap(r).wait_send()
    for g in range(groups):
        for name in ("a", "b", "y1", "y3e", "y3o", "d1", "d3", "d4", "d2"):
            sent(g, name)


def shards(sizes, query_rows, key_rows, value_rows, grad_rows, doc_ids):
    tokens, head_count, width = query_rows.shape
    groups = key_rows.shape[1]
    heads = head_count // groups
    me = lax.axis_index("ctx")
    own_ids = lax.dynamic_slice_in_dim(doc_ids, me * tokens, tokens, 0)
    first = jnp.sum((doc_ids[None, :] < own_ids[:, None]).astype(jnp.int32), axis=1)
    low = jnp.repeat(first - me * tokens, heads)[None, :]

    def by_group(x):
        return x.reshape(tokens, groups, heads, width).transpose(1, 0, 2, 3).reshape(groups, tokens * heads, width)

    def by_token(x):
        return x.reshape(groups, tokens, heads, width).transpose(1, 0, 2, 3).reshape(tokens, head_count, width)

    own = jnp.stack([key_rows, value_rows]).transpose(2, 0, 1, 3)
    tiles = REACH + 1
    keys = tiles * tokens
    rounds = sum((size - 1).bit_length() for size in sizes)
    vmem = pl.BlockSpec(memory_space=pltpu.VMEM)
    attended, query_grad, dkv, top = pl.pallas_call(
        functools.partial(kernel, heads, tokens, sizes),
        out_shape=(
            jax.ShapeDtypeStruct((groups, tokens * heads, width), BF16),
            jax.ShapeDtypeStruct((groups, tokens * heads, width), BF16),
            jax.ShapeDtypeStruct((groups, 2, tokens, width), BF16),
            jax.ShapeDtypeStruct((8, 128), F32),
        ),
        in_specs=[vmem] * 4,
        out_specs=(vmem,) * 4,
        scratch_shapes=[
            pltpu.VMEM((groups, tiles, 2, tokens, width), BF16),
            pltpu.VMEM((groups, REACH, 2, tokens, width), BF16),
            pltpu.VMEM((groups, REACH, 2, tokens, width), BF16),
            pltpu.VMEM((rounds, 8, 128), F32),
            pltpu.VMEM((rounds, 8, 128), F32),
            pltpu.VMEM((width, keys), BF16),
            pltpu.VMEM((width, keys), BF16),
            pltpu.VMEM((groups, keys, width), F32),
            pltpu.VMEM((groups, keys, width), F32),
            pltpu.VMEM((keys, tokens * heads), F32),
            pltpu.VMEM((keys, tokens * heads), F32),
            pltpu.VMEM((keys, tokens * heads), BF16),
            pltpu.VMEM((keys, tokens * heads), BF16),
            pltpu.VMEM((1, tokens * heads), F32),
            pltpu.VMEM((8, 128), F32),
            pltpu.SemaphoreType.DMA((groups, 9)),
            pltpu.SemaphoreType.DMA((groups, 9)),
            pltpu.SemaphoreType.DMA((rounds,)),
            pltpu.SemaphoreType.DMA((rounds,)),
        ],
        compiler_params=pltpu.CompilerParams(
            vmem_limit_bytes=50 << 20, collective_id=0, has_side_effects=True
        ),
    )(by_group(query_rows), by_group(grad_rows), low, own)
    result = dkv.transpose(1, 2, 0, 3)
    return by_token(attended), by_token(query_grad), result[0], result[1], top[0, 0]


def solution(mesh):
    part = P("ctx", "tp", None)
    return jax.shard_map(
        functools.partial(shards, (mesh.shape["ctx"], mesh.shape["tp"])),
        mesh=mesh,
        in_specs=(part, part, part, part, P()),
        out_specs=(part, part, part, part, P()),
        check_vma=False,
    )
```

```python
import functools
import math

import jax
import jax.numpy as jnp
from jax import lax
from jax.experimental import pallas as pl
from jax.experimental.pallas import tpu as pltpu
from jax.sharding import PartitionSpec as P

REACH = 4
ROWS = 256
FILL = 256
NEGATIVE = -1e30
F32 = jnp.float32
BF16 = jnp.bfloat16
NT = (((1,), (1,)), ((), ()))


def fill(g, j, heads, tokens, q_ref, do_ref, lo_ref, kv_ref, kt_ref, vt_ref, s_ref, dp_ref, max_ref):
    keys = pl.ds(j * tokens, tokens)
    kt_ref[:, keys] = kv_ref[g, j, 0].T
    vt_ref[:, keys] = kv_ref[g, j, 1].T
    key_place = lax.broadcasted_iota(jnp.int32, (tokens, FILL), 0)

    def body(c, carry):
        rows = pl.ds(pl.multiple_of(c * FILL, FILL), FILL)
        s = lax.dot_general(kv_ref[g, j, 0], q_ref[g, rows, :], NT, preferred_element_type=F32)
        allowed = key_place >= lo_ref[:, rows] + j * tokens
        if j == 0:
            query_place = (lax.broadcasted_iota(jnp.int32, (1, FILL), 1) + c * FILL) // heads
            allowed = allowed & (key_place <= query_place)
        s = jnp.where(allowed, s, NEGATIVE)
        s_ref[keys, rows] = s
        top = jnp.max(s, axis=0, keepdims=True)
        max_ref[:, rows] = top if j == 0 else jnp.maximum(max_ref[:, rows], top)
        dp_ref[keys, rows] = lax.dot_general(
            kv_ref[g, j, 1], do_ref[g, rows, :], NT, preferred_element_type=F32
        )
        return carry

    lax.fori_loop(0, q_ref.shape[1] // FILL, body, 0)


def chunk_step(
    c, g, tokens, o_ref, dq_ref, kt_ref, vt_ref, s_ref, dp_ref, w_ref, ds_ref, max_ref
):
    width = kt_ref.shape[0]
    tiles = kt_ref.shape[1] // tokens
    scale = 1.0 / math.sqrt(width)
    base2 = scale * math.log2(math.e)
    rows = pl.ds(pl.multiple_of(c * ROWS, ROWS), ROWS)
    top = max_ref[:, rows]
    total = jnp.zeros((1, ROWS), F32)
    dot = jnp.zeros((1, ROWS), F32)
    for j in range(tiles):
        keys = pl.ds(j * tokens, tokens)
        p = jnp.exp2((s_ref[keys, rows] - top) * base2)
        s_ref[keys, rows] = p
        total = total + jnp.sum(p, axis=0, keepdims=True)
        dot = dot + jnp.sum(p * dp_ref[keys, rows], axis=0, keepdims=True)
    inverse = 1.0 / total
    dot = dot * inverse
    for j in range(tiles):
        keys = pl.ds(j * tokens, tokens)
        p = s_ref[keys, rows] * inverse
        w_ref[keys, rows] = p.astype(BF16)
        ds_ref[keys, rows] = (p * (dp_ref[keys, rows] - dot)).astype(BF16)
    o = jnp.dot(vt_ref[...], w_ref[:, rows], preferred_element_type=F32)
    dq = jnp.dot(kt_ref[...], ds_ref[:, rows], preferred_element_type=F32) * scale
    o_ref[g, rows, :] = o.T.astype(BF16)
    dq_ref[g, rows, :] = dq.T.astype(BF16)


def kernel(
    heads, tokens, sizes, q_ref, do_ref, lo_ref, own_ref,
    o_ref, dq_ref, dkv_ref, top_ref,
    kv_ref, out_ref, back_ref, peak_ref, peer_ref, kt_ref, vt_ref, dk_ref, dv_ref,
    s_ref, dp_ref, w_ref, ds_ref, max_ref, best_ref, send_sem, recv_sem, peak_send, peak_recv,
):
    groups, rows, width = q_ref.shape
    ranks, lanes = sizes
    chunks = rows // ROWS
    scale = 1.0 / math.sqrt(width)
    me = lax.axis_index("ctx")
    lane = lax.axis_index("tp")
    odd = lax.rem(me, 2) == 1
    even = lax.rem(me, 2) == 0
    mate = me + 1 - 2 * lax.rem(me, 2)
    has_ahead = me + 2 < ranks

    def flip(index, bit):
        return index + bit - 2 * bit * lax.rem(index // bit, 2)

    peers = [("ctx", flip(me, 1 << b)) for b in range((ranks - 1).bit_length())]
    peers += [("tp", flip(lane, 1 << b)) for b in range((lanes - 1).bit_length())]
    barrier = pltpu.get_barrier_semaphore()

    def greet(axis, index):
        pl.semaphore_signal(barrier, inc=1, device_id={axis: index}, device_id_type=pl.DeviceIdType.MESH)

    for axis, index in peers:
        greet(axis, index)
    pl.when(has_ahead)(lambda: greet("ctx", me + 2))
    pl.when(me >= 2)(lambda: greet("ctx", me - 2))
    pl.semaphore_wait(barrier, len(peers) + has_ahead.astype(jnp.int32) + (me >= 2).astype(jnp.int32))

    def move(g, k, src, dst, target):
        return pltpu.make_async_remote_copy(
            src_ref=src, dst_ref=dst, send_sem=send_sem.at[g, k], recv_sem=recv_sem.at[g, k],
            device_id={"ctx": target}, device_id_type=pl.DeviceIdType.MESH,
        )

    def hops(g):
        kv = lambda j: kv_ref.at[g, j]
        out = lambda k: out_ref.at[g, k]
        back = lambda k: back_ref.at[g, k]
        return {
            "a": (0, [(has_ahead, own_ref.at[g])], kv(2), me + 2, me >= 2),
            "b": (1, [(has_ahead & (me >= 2), kv(2))], kv(4), me + 2, me >= 4),
            "y1": (2, [(even, own_ref.at[g]), (odd & (me >= 3), kv(2))], kv(1), mate, me >= 1),
            "y3e": (3, [(even & (me >= 2), kv(2))], kv(3), mate, odd & (me >= 3)),
            "y3o": (4, [(odd & (me >= 5), kv(4))], kv(3), mate, even & (me >= 4)),
            "d1": (5, [(me >= 1, out(0))], back(0), mate, even | (me >= 3)),
            "d3": (6, [(me >= 3, out(2))], back(2), mate, (even & (me >= 2)) | (me >= 5)),
            "d4": (7, [(me >= 4, out(3))], back(3), me - 2, has_ahead & (me >= 2)),
            "d2": (8, [(me >= 2, out(1))], back(1), me - 2, has_ahead),
        }

    def start(g, name):
        slot, sources, dst, target, _ = hops(g)[name]
        for cond, src in sources:
            pl.when(cond)(lambda src=src: move(g, slot, src, dst, target).start())

    def arrive(g, name):
        slot, sources, dst, target, cond = hops(g)[name]
        pl.when(cond)(lambda: move(g, slot, sources[0][1], dst, target).wait_recv())

    def sent(g, name):
        slot, sources, dst, target, _ = hops(g)[name]
        for cond, src in sources:
            pl.when(cond)(lambda src=src: move(g, slot, src, dst, target).wait_send())

    def add(k, cond, g, slot):
        keys = pl.ds(k * tokens, tokens)

        @pl.when(cond)
        def _():
            dk_ref[g, keys, :] += back_ref[g, slot, 0].astype(F32)
            dv_ref[g, keys, :] += back_ref[g, slot, 1].astype(F32)

    def pack(g, k):
        keys = pl.ds(k * tokens, tokens)
        out_ref[g, k - 1, 0] = dk_ref[g, keys, :].astype(BF16)
        out_ref[g, k - 1, 1] = dv_ref[g, keys, :].astype(BF16)

    def finish(g, j):
        keys = pl.ds(j * tokens, tokens)
        dv_ref[g, keys, :] = jnp.dot(w_ref[keys, :], do_ref[g], preferred_element_type=F32)
        dk_ref[g, keys, :] = jnp.dot(ds_ref[keys, :], q_ref[g], preferred_element_type=F32)

    def back_two(g):
        arrive(g, "d3")
        add(4, odd & (me >= 5), g, 2)
        pack(g, 4)
        start(g, "d4")

    def back_three(g):
        arrive(g, "d1")
        add(2, even & (me >= 2), g, 2)
        add(2, odd & (me >= 3), g, 0)
        arrive(g, "d4")
        add(2, has_ahead & (me >= 2), g, 3)
        pack(g, 2)
        start(g, "d2")

    def back_last(g):
        add(0, even, g, 0)
        arrive(g, "d2")
        add(0, has_ahead, g, 1)
        keys = pl.ds(0, tokens)
        dkv_ref[g, 0] = (dk_ref[g, keys, :] * scale).astype(BF16)
        dkv_ref[g, 1] = dv_ref[g, keys, :].astype(BF16)

    def begin(g):
        start(g, "a")
        pl.when(even)(lambda: move(g, 2, own_ref.at[g], kv_ref.at[g, 1], mate).start())

    def relay(g):
        arrive(g, "a")
        start(g, "b")
        pl.when(odd & (me >= 3))(lambda: move(g, 2, kv_ref.at[g, 2], kv_ref.at[g, 1], mate).start())
        start(g, "y3e")

    def relay_last(g):
        arrive(g, "b")
        start(g, "y3o")

    def swap(r):
        axis, index = peers[r]
        return pltpu.make_async_remote_copy(
            src_ref=peak_ref.at[r], dst_ref=peer_ref.at[r], send_sem=peak_send.at[r],
            recv_sem=peak_recv.at[r], device_id={axis: index}, device_id_type=pl.DeviceIdType.MESH,
        )

    def collect(r):
        if r > 0:
            swap(r - 1).wait_recv()
            best_ref[...] = jnp.maximum(best_ref[...], peer_ref[r - 1])
        if r < len(peers):
            peak_ref[r] = best_ref[...]
            swap(r).start()

    def fill_tile(g, j):
        fill(g, j, heads, tokens, q_ref, do_ref, lo_ref, kv_ref, kt_ref, vt_ref, s_ref, dp_ref, max_ref)

    def note_peak():
        best = jnp.max(max_ref[...], axis=1, keepdims=True) * scale
        best_ref[...] = jnp.maximum(best_ref[...], jnp.broadcast_to(best, best_ref.shape))

    def main(g, plan):
        def step(c, carry):
            for at, works in plan.items():
                @pl.when(c == at)
                def _(works=works):
                    for work in works:
                        work()
            chunk_step(c, g, tokens, o_ref, dq_ref, kt_ref, vt_ref, s_ref, dp_ref, w_ref, ds_ref, max_ref)
            return carry

        lax.fori_loop(0, chunks, step, 0)

    begin(0)
    best_ref[...] = jnp.full_like(best_ref, NEGATIVE)
    for g in range(groups):
        kv_ref[g, 0] = own_ref[g]
        for j in range(1, REACH + 1):
            @pl.when(me < j)
            def _(g=g, j=j):
                kv_ref[g, j] = jnp.zeros_like(kv_ref[g, j])
    last = groups - 1
    for g in range(groups):
        fill_tile(g, 0)
        if g == 0:
            relay(0)
            fill_tile(0, 2)
            arrive(0, "y1")
            fill_tile(0, 1)
            relay_last(0)
            if last > 0:
                begin(1)
            fill_tile(0, 4)
            arrive(0, "y3e")
            arrive(0, "y3o")
            fill_tile(0, 3)
        else:
            fill_tile(g, 2)
            arrive(g, "y1")
            fill_tile(g, 1)
            back_two(g - 1)
            fill_tile(g, 4)
            arrive(g, "y3e")
            arrive(g, "y3o")
            fill_tile(g, 3)
        note_peak()
        plan = {}
        if g > 0:
            plan.setdefault(1, []).append(lambda g=g: back_three(g - 1))
            plan.setdefault(4, []).append(lambda g=g: back_last(g - 1))
        if g < last:
            plan.setdefault(2, []).append(lambda g=g: relay(g + 1))
            plan.setdefault(5, []).append(lambda g=g: relay_last(g + 1))
            if g + 1 < last:
                plan.setdefault(6, []).append(lambda g=g: begin(g + 2))
        else:
            for r in range(min(len(peers) + 1, chunks)):
                plan.setdefault(r, []).append(lambda r=r: collect(r))
        main(g, plan)
        finish(g, 3)
        pack(g, 3)
        start(g, "d3")
        finish(g, 1)
        pack(g, 1)
        finish(g, 4)
        finish(g, 2)
        if g == last:
            back_two(g)
        start(g, "d1")
        finish(g, 0)
        if g == last:
            back_three(g)
    for r in range(chunks, len(peers) + 1):
        collect(r)
    top_ref[...] = best_ref[...]
    back_last(last)
    for r in range(len(peers)):
        swap(r).wait_send()
    for g in range(groups):
        for name in ("a", "b", "y1", "y3e", "y3o", "d1", "d3", "d4", "d2"):
            sent(g, name)


def shards(sizes, query_rows, key_rows, value_rows, grad_rows, doc_ids):
    tokens, head_count, width = query_rows.shape
    groups = key_rows.shape[1]
    heads = head_count // groups
    me = lax.axis_index("ctx")
    own_ids = lax.dynamic_slice_in_dim(doc_ids, me * tokens, tokens, 0)
    first = jnp.sum((doc_ids[None, :] < own_ids[:, None]).astype(jnp.int32), axis=1)
    low = jnp.repeat(first - me * tokens, heads)[None, :]

    def by_group(x):
        return x.reshape(tokens, groups, heads, width).transpose(1, 0, 2, 3).reshape(groups, tokens * heads, width)

    def by_token(x):
        return x.reshape(groups, tokens, heads, width).transpose(1, 0, 2, 3).reshape(tokens, head_count, width)

    own = jnp.stack([key_rows, value_rows]).transpose(2, 0, 1, 3)
    tiles = REACH + 1
    keys = tiles * tokens
    rounds = sum((size - 1).bit_length() for size in sizes)
    vmem = pl.BlockSpec(memory_space=pltpu.VMEM)
    attended, query_grad, dkv, top = pl.pallas_call(
        functools.partial(kernel, heads, tokens, sizes),
        out_shape=(
            jax.ShapeDtypeStruct((groups, tokens * heads, width), BF16),
            jax.ShapeDtypeStruct((groups, tokens * heads, width), BF16),
            jax.ShapeDtypeStruct((groups, 2, tokens, width), BF16),
            jax.ShapeDtypeStruct((8, 128), F32),
        ),
        in_specs=[vmem] * 4,
        out_specs=(vmem,) * 4,
        scratch_shapes=[
            pltpu.VMEM((groups, tiles, 2, tokens, width), BF16),
            pltpu.VMEM((groups, REACH, 2, tokens, width), BF16),
            pltpu.VMEM((groups, REACH, 2, tokens, width), BF16),
            pltpu.VMEM((rounds, 8, 128), F32),
            pltpu.VMEM((rounds, 8, 128), F32),
            pltpu.VMEM((width, keys), BF16),
            pltpu.VMEM((width, keys), BF16),
            pltpu.VMEM((groups, keys, width), F32),
            pltpu.VMEM((groups, keys, width), F32),
            pltpu.VMEM((keys, tokens * heads), F32),
            pltpu.VMEM((keys, tokens * heads), F32),
            pltpu.VMEM((keys, tokens * heads), BF16),
            pltpu.VMEM((keys, tokens * heads), BF16),
            pltpu.VMEM((1, tokens * heads), F32),
            pltpu.VMEM((8, 128), F32),
            pltpu.SemaphoreType.DMA((groups, 9)),
            pltpu.SemaphoreType.DMA((groups, 9)),
            pltpu.SemaphoreType.DMA((rounds,)),
            pltpu.SemaphoreType.DMA((rounds,)),
        ],
        compiler_params=pltpu.CompilerParams(
            vmem_limit_bytes=50 << 20, collective_id=0, has_side_effects=True
        ),
    )(by_group(query_rows), by_group(grad_rows), low, own)
    result = dkv.transpose(1, 2, 0, 3)
    return by_token(attended), by_token(query_grad), result[0], result[1], top[0, 0]


def solution(mesh):
    part = P("ctx", "tp", None)
    return jax.shard_map(
        functools.partial(shards, (mesh.shape["ctx"], mesh.shape["tp"])),
        mesh=mesh,
        in_specs=(part, part, part, part, P()),
        out_specs=(part, part, part, part, P()),
        check_vma=False,
    )
```
